512 devices in a mesh: grp: 16 (over z, core), edge: 32 (over x, y).
Axes of the slice: x: 4, y: 8, z: 8, core: 2. Of those that a mesh axis runs over, the one named last changes fastest.
Arguments:
- grad_out: bfloat16 [65536, 256], P(('grp', 'edge')), may hold values from -6 to 6
- in_degree: int32 [65536], P(('grp', 'edge')), may hold values from 4 to 16
- w_self: bfloat16 [256, 256], replicated, may hold values from -0.375 to 0.375
- w_neigh: bfloat16 [256, 256], replicated, may hold values from -0.375 to 0.375
- block_dst_tile: int32 [131072], P(('grp', 'edge')), may hold values from 0 to 31
- block_src_group: int32 [131072], P(('grp', 'edge')), may hold values from 0 to 15
- edge_dst: int32 [131072, 128], P(('grp', 'edge')), may hold values from 0 to 127
- edge_src: int32 [131072, 128], P(('grp', 'edge')), may hold values from 0 to 127
- block_count: int32 [512], P(('grp', 'edge')), may hold values from 64 to 256, as said below
- mirror_tiles: int32 [512, 16], P(('grp', 'edge')), may hold values from 0 to 31
Outputs:
- grad_feats: bfloat16 [65536, 256], P(('grp', 'edge'))
- mirror_grads: bfloat16 [512, 16, 128, 256], P(('grp', 'edge'))
The draws below stay inside these ranges and needn't reach their ends.
Inputs may be any that keep to these rules, and one draw needn't show every extreme that they name: The live slots of a device are its first block_count ones; in every group one device has all 256 slots live.
All inputs are finite; a program needn't handle non-finite values.
Results may differ from the reference program's by a relative error of at most 0.0043.
Values may be sent and summed in bfloat16 or wider, within the bound.
A program may use at most 64 MiB of HBM per device.

```python
import jax
import jax.numpy as jnp
from jax import lax

D = 256
TILE = 128
B_DEV = 256
GROUPS = 16
GROUP_DEVS = 32
DEVICE_COUNT = 512
TILES_GRP = 32
VERTS = 65536
BLOCKS = 131072


def draw_block_count(key, part):
    key = jax.random.fold_in(key, 7)
    key_base, key_hub = jax.random.split(key)
    base_counts = jax.random.randint(key_base, (GROUPS, GROUP_DEVS), B_DEV // 4, B_DEV * 5 // 8 + 1)
    hub_index = jax.random.randint(key_hub, (GROUPS, 1), 0, GROUP_DEVS)
    is_hub = jnp.arange(GROUP_DEVS, dtype=jnp.int32)[None, :] == hub_index
    return jnp.where(is_hub, B_DEV, base_counts).reshape(-1).astype(jnp.int32)


def with_ends(values, rng, least, high):
    dims = values.shape
    spot = [jax.random.randint(jax.random.fold_in(rng, axis), (), 0, dims[axis]) for axis in range(len(dims))]
    values = values.at[tuple(spot)].set(least)
    longest = dims.index(max(dims))
    spot[longest] = (spot[longest] + 1) % dims[longest]
    return values.at[tuple(spot)].set(high)


def block_levels(rng, shape, shards, least, largest):
    factor_of, own = 1.0, jax.random.fold_in(rng, 6)
    for dim, parts in shards:
        heights = jnp.exp(jax.random.uniform(jax.random.fold_in(own, dim), (parts,), jnp.float32, least / len(shards), largest / len(shards)))
        factor_of = factor_of * jnp.repeat(heights, shape[dim] // parts).reshape([-1 if axis == dim else 1 for axis in range(len(shape))])
    return factor_of


def bell_draw(key, dims, width, most, cuts=(), kind=jnp.bfloat16):
    entries = width * jax.random.normal(key, dims, jnp.float32)
    if cuts:
        entries = entries * block_levels(key, dims, cuts, -0.22, 0.18)
    return jnp.clip(entries, -most, most).astype(kind)


def setup_inputs(seed: int = 0) -> dict:
    keys = jax.random.split(jax.random.key(seed), 11)
    return {
        "grad_out": bell_draw(keys[0], (VERTS, D), 1.0, 6.0, ((0, 512),)),
        "in_degree": with_ends(jax.random.randint(keys[1], (VERTS,), 4, 17), jax.random.fold_in(keys[1], 1), 4, 16).astype(jnp.int32),
        "w_self": bell_draw(keys[2], (D, D), D ** -0.5, 0.375),
        "w_neigh": bell_draw(keys[3], (D, D), D ** -0.5, 0.375),
        "block_dst_tile": with_ends(jax.random.randint(keys[4], (BLOCKS,), 0, TILES_GRP), jax.random.fold_in(keys[4], 1), 0, TILES_GRP - 1).astype(jnp.int32),
        "block_src_group": with_ends(jax.random.randint(keys[5], (BLOCKS,), 0, GROUPS), jax.random.fold_in(keys[5], 1), 0, GROUPS - 1).astype(jnp.int32),
        "edge_dst": with_ends(jax.random.randint(keys[6], (BLOCKS, TILE), 0, TILE), jax.random.fold_in(keys[6], 1), 0, TILE - 1).astype(jnp.int32),
        "edge_src": with_ends(jax.random.randint(keys[7], (BLOCKS, TILE), 0, TILE), jax.random.fold_in(keys[7], 1), 0, TILE - 1).astype(jnp.int32),
        "block_count": draw_block_count(jax.random.fold_in(keys[10], 71), 0),
        "mirror_tiles": with_ends(jax.random.randint(keys[9], (DEVICE_COUNT, GROUPS), 0, TILES_GRP), jax.random.fold_in(keys[9], 1), 0, TILES_GRP - 1).astype(jnp.int32),
    }


def reference(grad_out, in_degree, w_self, w_neigh, block_dst_tile, block_src_group, edge_dst, edge_src, block_count, mirror_tiles):
    self_term = jnp.dot(grad_out, w_self.T, preferred_element_type=jnp.float32)
    neigh_grad = jnp.dot(grad_out, w_neigh.T, preferred_element_type=jnp.float32)
    messages = (neigh_grad / in_degree.astype(jnp.float32)[:, None]).astype(jnp.bfloat16)
    messages = lax.optimization_barrier(messages).astype(jnp.float32)
    group_rows = TILES_GRP * TILE

    def one_device(totals, device):
        first_block = device * B_DEV
        dst_tile = lax.dynamic_slice_in_dim(block_dst_tile, first_block, B_DEV)
        src_group = lax.dynamic_slice_in_dim(block_src_group, first_block, B_DEV)
        rows_dst = lax.dynamic_slice_in_dim(edge_dst, first_block, B_DEV, 0)
        rows_src = lax.dynamic_slice_in_dim(edge_src, first_block, B_DEV, 0)
        live_mask = (jnp.arange(B_DEV, dtype=jnp.int32) < block_count[device]).astype(jnp.float32)
        mirrors = mirror_tiles[device]
        home_group = device // GROUP_DEVS
        dst_global = home_group * group_rows + dst_tile[:, None] * TILE + rows_dst
        src_global = src_group[:, None] * group_rows + mirrors[src_group][:, None] * TILE + rows_src
        arrivals = messages[dst_global.reshape(-1)] * jnp.repeat(live_mask, TILE)[:, None]
        return totals.at[src_global.reshape(-1)].add(arrivals), None

    neighbour, unused = lax.scan(one_device, jnp.zeros(self_term.shape, jnp.float32), jnp.arange(DEVICE_COUNT, dtype=jnp.int32))
    grad_feats = (self_term + neighbour).astype(jnp.bfloat16)
    tiles_all = grad_feats.reshape(-1, TILE, grad_feats.shape[1])
    picked = jnp.arange(GROUPS, dtype=jnp.int32)[None, :] * TILES_GRP + mirror_tiles
    mirror_grads = tiles_all[picked]
    return grad_feats, mirror_grads
```

```python
import functools

import jax
import jax.numpy as jnp
from jax import lax
from jax.experimental import pallas as pl
from jax.experimental.pallas import tpu as pltpu
from jax.sharding import PartitionSpec as P

MESH = pl.DeviceIdType.MESH
NX, NY = 4, 8
NE = NX * NY
NG = 16
TILE = 128
D = 256
H = 128
B = 256
CHUNKS = 4
R = TILE // CHUNKS
MB = 1024 * 1024
F32 = jnp.float32
BF16 = jnp.bfloat16
NT = (((1,), (1,)), ((), ()))


def here():
    e = lax.axis_index("edge")
    return lax.div(e, NY), lax.rem(e, NY)


def wrap_x(x):
    return lax.rem(x + 2 * NX, NX)


def wrap_y(y):
    return lax.rem(y + 2 * NY, NY)


def node(x, y):
    return {"edge": wrap_x(x) * NY + wrap_y(y)}


def ring_peers():
    x, y = here()
    return [node(x + 1, y), node(x - 1, y), node(x, y + 1), node(x, y - 1)]


def greet(z_peers):
    barrier = pltpu.get_barrier_semaphore()
    for peer in ring_peers():
        pl.semaphore_signal(barrier, inc=1, device_id=peer, device_id_type=MESH)
    count = 4
    if z_peers:
        me = lax.axis_index("grp")

        def signal(i, carry):
            pl.semaphore_signal(
                barrier, inc=1, device_id={"grp": lax.rem(me + i, NG)}, device_id_type=MESH
            )
            return carry

        lax.fori_loop(1, NG, signal, 0)
        count += NG - 1
    pl.semaphore_wait(barrier, count)


def gather_copies(fa, fb, send, recv):
    x, y = here()
    rows = fa.shape[1]
    half_rows = rows // 2
    out = [[], []]
    for k in range(6):
        row_a, row_b = [], []
        for d, sign in enumerate((1, -1)):
            half = pl.ds(d * half_rows, half_rows)
            if k == 0:
                a = fa.at[pl.ds(y * NX + x, 1)]
            elif k == 1:
                a = fa.at[pl.ds(y * NX + wrap_x(x - sign), 1), half]
            elif k < 5:
                a = fa.at[pl.ds(wrap_y(y - (k - 2) * sign) * NX, NX)]
            else:
                a = fa.at[pl.ds(wrap_y(y - 3 * sign) * NX + d * (NX // 2), NX // 2)]
            to_a = node(x + sign, y) if k < 2 else node(x, y + sign)
            if k < 3:
                b = fb.at[pl.ds(x * NY + wrap_y(y - k * sign), 1)]
            elif k == 3:
                b = fb.at[pl.ds(x * NY + wrap_y(y - 3 * sign), 1), half]
            elif k == 4:
                b = fb.at[pl.ds(x * NY, NY)]
            else:
                b = fb.at[pl.ds(wrap_x(x - sign) * NY + d * (NY // 2), NY // 2)]
            to_b = node(x, y + sign) if k < 4 else node(x + sign, y)
            for color, ref, to, row in ((0, a, to_a, row_a), (1, b, to_b, row_b)):
                row.append(
                    pltpu.make_async_remote_copy(
                        src_ref=ref,
                        dst_ref=ref,
                        send_sem=send.at[color, k, d],
                        recv_sem=recv.at[color, k, d],
                        device_id=to,
                        device_id_type=MESH,
                    )
                )
        out[0].append(row_a)
        out[1].append(row_b)
    return out


def gather_stage(copies, stage):
    for color in range(2):
        if stage > 0:
            for c in copies[color][stage - 1]:
                c.wait_recv()
        if stage < 6:
            for c in copies[color][stage]:
                c.start()


def gather_finish(copies):
    for color in range(2):
        for row in copies[color]:
            for c in row:
                c.wait_send()


def gather_kernel(
    g_ref, deg_ref, w_ref, es_ref, ed_ref, mt_ref,
    ma_ref, mb_ref, counts_ref, ids_ref,
    held, send, recv, id_send, id_recv, out_sem,
):
    x, y = here()
    me = lax.axis_index("grp")
    ids_ref[pl.ds(me, 1)] = jnp.zeros((1, 8, 128), jnp.int32)
    ids_ref[pl.ds(me, 1), 0:1, 0:NG] = mt_ref[...].reshape(1, 1, NG)
    neigh = lax.dot_general(g_ref[...], w_ref[...], NT, preferred_element_type=F32)
    deg = jnp.broadcast_to(deg_ref[...].astype(F32), (TILE, TILE)).T
    ma_ref[pl.ds(y * NX + x, 1)] = (neigh[:, :H] / deg).astype(BF16)[None]
    mb_ref[pl.ds(x * NY + y, 1)] = (neigh[:, H:] / deg).astype(BF16)[None]
    greet(True)

    copies = gather_copies(ma_ref, mb_ref, send, recv)
    rows_id = lax.broadcasted_iota(jnp.int32, (TILE, TILE), 0)

    def id_copy(i):
        peer = lax.rem(me + i, NG)
        return pltpu.make_async_remote_copy(
            src_ref=ids_ref.at[pl.ds(me, 1)],
            dst_ref=ids_ref.at[pl.ds(me, 1)],
            send_sem=id_send.at[i],
            recv_sem=id_recv.at[i],
            device_id={"grp": peer},
            device_id_type=MESH,
        )

    def one(b):
        src = (rows_id == es_ref[pl.ds(b, 1), :]).astype(F32).astype(BF16)
        dst = (rows_id == ed_ref[pl.ds(b, 1), :]).astype(F32).astype(BF16)
        held[pl.ds(b, 1)] = lax.dot_general(
            src, dst, NT, preferred_element_type=F32
        ).astype(BF16)[None]

    per_part = B // 8

    def build(part):
        def body(i, carry):
            b = part * per_part + i * 4
            for j in range(4):
                one(b + j)
            return carry

        lax.fori_loop(0, per_part // 4, body, 0)
        span = pl.ds(part * per_part, per_part)
        copy = pltpu.make_async_copy(held.at[span], counts_ref.at[span], out_sem.at[part])
        copy.start()
        return copy

    outs = []
    for stage in range(7):
        gather_stage(copies, stage)
        if stage == 0:
            def start_id(i, carry):
                id_copy(i).start()
                return carry
            lax.fori_loop(1, NG, start_id, 0)
        if stage < 6:
            outs.append(build(stage))
        if stage in (1, 3):
            outs.append(build(6 + stage // 2))

    def end_id(i, carry):
        id_copy(i).wait()
        return carry

    lax.fori_loop(1, NG, end_id, 0)
    gather_finish(copies)
    for copy in outs:
        copy.wait()


def gather(grad_out, deg, w_neigh, edge_src, edge_dst, mirror_tiles):
    vmem = pl.BlockSpec(memory_space=pltpu.VMEM)
    return pl.pallas_call(
        gather_kernel,
        out_shape=(
            jax.ShapeDtypeStruct((NE, TILE, H), BF16),
            jax.ShapeDtypeStruct((NE, TILE, H), BF16),
            jax.ShapeDtypeStruct((B, TILE, TILE), BF16),
            jax.ShapeDtypeStruct((NG, 8, 128), jnp.int32),
        ),
        in_specs=[vmem] * 6,
        out_specs=(vmem, vmem, pl.BlockSpec(memory_space=pl.ANY), vmem),
        scratch_shapes=[
            pltpu.VMEM((B, TILE, TILE), BF16),
            pltpu.SemaphoreType.DMA((2, 6, 2)),
            pltpu.SemaphoreType.DMA((2, 6, 2)),
            pltpu.SemaphoreType.DMA((NG,)),
            pltpu.SemaphoreType.DMA((NG,)),
            pltpu.SemaphoreType.DMA((8,)),
        ],
        compiler_params=pltpu.CompilerParams(
            collective_id=0, has_side_effects=True, vmem_limit_bytes=32 * MB
        ),
        name="gather_messages",
    )(grad_out, deg, w_neigh, edge_src, edge_dst, mirror_tiles)


def sum_kernel(
    dt_ref, sg_ref, live_ref, ids_ref, counts_ref, ma_ref, mb_ref,
    part_ref, prev_ref, last_ref, tid_ref,
    held, head, size, nxt, sem,
):
    pieces = 8
    span = B // pieces
    copies = [
        pltpu.make_async_copy(
            counts_ref.at[pl.ds(p * span, span)], held.at[pl.ds(p * span, span)], sem.at[p]
        )
        for p in range(pieces)
    ]
    for c in copies:
        c.start()

    me = lax.axis_index("grp")

    def clear(t, carry):
        last_ref[t] = NG
        return carry

    lax.fori_loop(0, NE, clear, 0)

    def link(g, carry):
        t = ids_ref[g, 0, me]
        tid_ref[g] = t
        prev_ref[g] = last_ref[t]
        last_ref[t] = g
        return carry

    lax.fori_loop(0, NG, link, 0)

    def reset(s, carry):
        head[s] = 0
        size[s] = 0
        return carry

    lax.fori_loop(0, NG, reset, 0)

    def chain(b, carry):
        s = sg_ref[b]
        nxt[b] = head[s]
        head[s] = b
        size[s] = size[s] + 1
        return carry

    lax.fori_loop(0, live_ref[0], chain, 0)
    for c in copies:
        c.wait()

    def tile_of(b):
        t = dt_ref[b]
        ia = lax.rem(t, NY) * NX + lax.div(t, NY)
        return jnp.concatenate([ma_ref[ia], mb_ref[t]], axis=1)

    def group(s, carry):
        n = size[s]

        def pair(i, state):
            b1, acc = state
            b2 = nxt[b1]
            both = (2 * i + 1) < n
            second = jnp.where(both, held[b2], jnp.zeros((TILE, TILE), BF16))
            lhs = jnp.concatenate([held[b1], second], axis=1)
            rhs = jnp.concatenate([tile_of(b1), tile_of(b2)], axis=0)
            acc = acc + jnp.dot(lhs, rhs, preferred_element_type=F32)
            return nxt[b2], acc

        state = lax.fori_loop(
            0, lax.div(n + 1, 2), pair, (head[s], jnp.zeros((TILE, D), F32))
        )
        acc = state[1].astype(BF16)
        for c in range(CHUNKS):
            for h in range(2):
                part_ref[c, s, h] = acc[c * R : (c + 1) * R, h * H : (h + 1) * H]
        return carry

    lax.fori_loop(0, NG, group, 0)


def edge_sums(dst_tile, src_group, count, ids, counts, ma, mb):
    smem = pl.BlockSpec(memory_space=pltpu.SMEM)
    vmem = pl.BlockSpec(memory_space=pltpu.VMEM)
    return pl.pallas_call(
        sum_kernel,
        out_shape=(
            jax.ShapeDtypeStruct((CHUNKS, NG, 2, R, H), BF16),
            jax.ShapeDtypeStruct((NG,), jnp.int32),
            jax.ShapeDtypeStruct((NE,), jnp.int32),
            jax.ShapeDtypeStruct((NG,), jnp.int32),
        ),
        in_specs=[smem] * 4 + [pl.BlockSpec(memory_space=pl.ANY), vmem, vmem],
        out_specs=(vmem, smem, smem, smem),
        scratch_shapes=[
            pltpu.VMEM((B, TILE, TILE), BF16),
            pltpu.SMEM((NG,), jnp.int32),
            pltpu.SMEM((NG,), jnp.int32),
            pltpu.SMEM((B,), jnp.int32),
            pltpu.SemaphoreType.DMA((8,)),
        ],
        compiler_params=pltpu.CompilerParams(vmem_limit_bytes=32 * MB),
        name="edge_sums",
    )(dst_tile, src_group, count, ids, counts, ma, mb)


Z_ORDER = (8, 9, 7, 6, 10, 5, 11, 4, 12, 3, 13, 2, 14, 1, 15)


def merge_kernel(
    part_ref, prev_ref, last_ref, tid_ref, g_ref, w_ref,
    gf_ref, mg_ref,
    self_term, own_sem, z_send, z_recv, r_send, r_recv, f_send, f_recv, b_send, b_recv,
    *bufs,
):
    x, y = here()
    me = lax.axis_index("grp")
    names = (
        "relay", "sums", "sa0", "sa", "ra0", "ra", "ua", "ra4", "sa5", "ra5",
        "sb0", "sb1", "rb0", "rb1", "ub", "rb2", "sb", "rb", "fa", "fb", "picked",
    )
    per = len(names)
    chunks = [dict(zip(names, bufs[c * per : (c + 1) * per])) for c in range(CHUNKS)]

    greet(True)

    def z_copy(c, i):
        peer = lax.rem(me + i, NG)
        return pltpu.make_async_remote_copy(
            src_ref=part_ref.at[c, peer],
            dst_ref=chunks[c]["relay"].at[me],
            send_sem=z_send.at[c, i],
            recv_sem=z_recv.at[c, i],
            device_id={"grp": peer},
            device_id_type=MESH,
        )

    def own_copy(c):
        return pltpu.make_async_copy(
            part_ref.at[c, me], chunks[c]["relay"].at[me], own_sem.at[c]
        )

    for c in range(CHUNKS):
        own_copy(c).start()
        for i in Z_ORDER:
            z_copy(c, i).start()

    self_term[...] = lax.dot_general(g_ref[...], w_ref[...], NT, preferred_element_type=F32)

    def ring(c, color, k, d, src, dst):
        sign = 1 - 2 * d
        along_y = (k < 4) if color == 0 else (k >= 2)
        return pltpu.make_async_remote_copy(
            src_ref=src,
            dst_ref=dst,
            send_sem=r_send.at[c, color, k, d],
            recv_sem=r_recv.at[c, color, k, d],
            device_id=node(x, y + sign) if along_y else node(x + sign, y),
            device_id_type=MESH,
        )

    half_rows = R // 2

    def ring_copy(c, color, k, d):
        buf = chunks[c]
        half = pl.ds(d * half_rows, half_rows)
        if color == 0:
            if k == 0:
                src, dst = buf["sa0"].at[d], buf["ra0"].at[d]
            elif k < 4:
                src, dst = buf["sa"].at[k - 1, d], buf["ra"].at[k - 1, d]
            elif k == 4:
                src, dst = buf["ua"].at[wrap_x(x + 2), half], buf["ra4"].at[d]
            else:
                src, dst = buf["sa5"].at[d], buf["ra5"].at[d]
        else:
            if k == 0:
                src, dst = buf["sb0"].at[d], buf["rb0"].at[d]
            elif k == 1:
                src, dst = buf["sb1"].at[d], buf["rb1"].at[d]
            elif k == 2:
                src, dst = buf["ub"].at[wrap_y(y + 4), half], buf["rb2"].at[d]
            else:
                src, dst = buf["sb"].at[k - 3, d], buf["rb"].at[k - 3, d]
        return ring(c, color, k, d, src, dst)

    def tile_sum(c, color, xx, yy):
        return chunks[c]["sums"][last_ref[xx * NY + yy], color]

    def relay_stage(c):
        buf = chunks[c]
        own_copy(c).wait()

        def arrive(i, carry):
            z_copy(c, i).wait_recv()
            return carry

        lax.fori_loop(1, NG, arrive, 0)
        buf["sums"][NG] = jnp.zeros((2, R, H), F32)

        def add(g, carry):
            buf["sums"][g] = buf["relay"][g].astype(F32) + buf["sums"][prev_ref[g]]
            return carry

        for g in range(NG):
            add(g, 0)

    def reduce_a(c, k):
        buf = chunks[c]
        if k > 0:
            for d in range(2):
                ring_copy(c, 0, k - 1, d).wait_recv()
        if k == 0:
            for d in range(2):
                for j in range(2):
                    buf["sa0"][d, j] = tile_sum(c, 0, 2 * d + j, wrap_y(y + 4)).astype(BF16)
        elif k < 4:
            for d in range(2):
                yy = wrap_y(y + (4 - k) * (1 - 2 * d))
                for xx in range(NX):
                    v = tile_sum(c, 0, xx, yy)
                    if k > 1:
                        v = v + buf["ra"][k - 2, d, xx].astype(F32)
                    elif xx // 2 == d:
                        v = v + buf["ra0"][d, xx % 2].astype(F32)
                    buf["sa"][k - 1, d, xx] = v.astype(BF16)
        elif k == 4:
            for xx in range(NX):
                buf["ua"][xx] = (
                    tile_sum(c, 0, xx, y)
                    + buf["ra"][2, 0, xx].astype(F32)
                    + buf["ra"][2, 1, xx].astype(F32)
                )
        elif k == 5:
            for d in range(2):
                xx = wrap_x(x + 1 - 2 * d)
                buf["sa5"][d] = buf["ua"][xx]
                half = pl.ds(d * half_rows, half_rows)
                buf["sa5"][d, half] = buf["sa5"][d, half] + buf["ra4"][d]
        else:
            return buf["ua"][x] + buf["ra5"][0] + buf["ra5"][1]
        for d in range(2):
            ring_copy(c, 0, k, d).start()
        return None

    def reduce_b(c, k):
        buf = chunks[c]
        if k > 0:
            for d in range(2):
                ring_copy(c, 1, k - 1, d).wait_recv()
        if k == 0:
            for d in range(2):
                for j in range(4):
                    buf["sb0"][d, j] = tile_sum(c, 1, wrap_x(x + 2), 4 * d + j).astype(BF16)
        elif k == 1:
            for d in range(2):
                xx = wrap_x(x + 1 - 2 * d)
                for yy in range(NY):
                    v = tile_sum(c, 1, xx, yy)
                    if yy // 4 == d:
                        v = v + buf["rb0"][d, yy % 4].astype(F32)
                    buf["sb1"][d, yy] = v.astype(BF16)
        elif k == 2:
            for yy in range(NY):
                buf["ub"][yy] = (
                    tile_sum(c, 1, x, yy)
                    + buf["rb1"][0, yy].astype(F32)
                    + buf["rb1"][1, yy].astype(F32)
                )
        elif k < 6:
            for d in range(2):
                yy = wrap_y(y + (6 - k) * (1 - 2 * d))
                if k == 3:
                    buf["sb"][0, d] = buf["ub"][yy]
                    half = pl.ds(d * half_rows, half_rows)
                    buf["sb"][0, d, half] = buf["sb"][0, d, half] + buf["rb2"][d]
                else:
                    buf["sb"][k - 3, d] = buf["ub"][yy] + buf["rb"][k - 4, d]
        else:
            return buf["ub"][y] + buf["rb"][2, 0] + buf["rb"][2, 1]
        for d in range(2):
            ring_copy(c, 1, k, d).start()
        return None

    gathers = [
        gather_copies(chunks[c]["fa"], chunks[c]["fb"], f_send.at[c], f_recv.at[c])
        for c in range(CHUNKS)
    ]

    def back_copy(c, i):
        peer = lax.rem(me + i, NG)
        return pltpu.make_async_remote_copy(
            src_ref=chunks[c]["picked"].at[peer],
            dst_ref=mg_ref.at[0, me, pl.ds(c * R, R)],
            send_sem=b_send.at[c, i],
            recv_sem=b_recv.at[c, i],
            device_id={"grp": peer},
            device_id_type=MESH,
        )

    def back_own(c):
        return pltpu.make_async_copy(
            chunks[c]["picked"].at[me], mg_ref.at[0, me, pl.ds(c * R, R)], own_sem.at[CHUNKS + c]
        )

    def finish_tile(c):
        buf = chunks[c]
        own_a = reduce_a(c, 6)
        own_b = reduce_b(c, 6)
        rows = pl.ds(c * R, R)
        out_a = (self_term[rows, 0:H] + own_a).astype(BF16)
        out_b = (self_term[rows, H:D] + own_b).astype(BF16)
        gf_ref[rows, 0:H] = out_a
        gf_ref[rows, H:D] = out_b
        buf["fa"][pl.ds(y * NX + x, 1)] = out_a[None]
        buf["fb"][pl.ds(x * NY + y, 1)] = out_b[None]
        gather_stage(gathers[c], 0)

    def send_back(c):
        buf = chunks[c]
        gather_stage(gathers[c], 6)
        for g in range(NG):
            t = tid_ref[g]
            ia = lax.rem(t, NY) * NX + lax.div(t, NY)
            buf["picked"][g, :, 0:H] = buf["fa"][ia]
            buf["picked"][g, :, H:D] = buf["fb"][t]
        back_own(c).start()
        for i in Z_ORDER:
            back_copy(c, i).start()

    stages = []
    for k in range(6):
        def reduce_step(c, k=k):
            if k == 0:
                relay_stage(c)
            reduce_a(c, k)
            reduce_b(c, k)
        stages.append(reduce_step)
    stages.append(finish_tile)
    for k in range(1, 6):
        stages.append(lambda c, k=k: gather_stage(gathers[c], k))
    stages.append(send_back)

    lag = 3
    for tick in range(len(stages) + lag * (CHUNKS - 1)):
        for c in range(CHUNKS):
            k = tick - lag * c
            if 0 <= k < len(stages):
                stages[k](c)

    for c in range(CHUNKS):
        back_own(c).wait()

        def end(i, carry, c=c):
            z_copy(c, i).wait_send()
            back_copy(c, i).wait()
            return carry

        lax.fori_loop(1, NG, end, 0)
        for color in range(2):
            for k in range(6):
                for d in range(2):
                    ring_copy(c, color, k, d).wait_send()
        gather_finish(gathers[c])


def merge(part, prev, last, tid, grad_out, w_self):
    smem = pl.BlockSpec(memory_space=pltpu.SMEM)
    vmem = pl.BlockSpec(memory_space=pltpu.VMEM)
    hbm = pl.BlockSpec(memory_space=pl.ANY)
    half = R // 2
    per_chunk = [
        pltpu.VMEM((NG, 2, R, H), BF16),
        pltpu.VMEM((NG + 1, 2, R, H), F32),
        pltpu.VMEM((2, 2, R, H), BF16),
        pltpu.VMEM((3, 2, NX, R, H), BF16),
        pltpu.VMEM((2, 2, R, H), BF16),
        pltpu.VMEM((3, 2, NX, R, H), BF16),
        pltpu.VMEM((NX, R, H), F32),
        pltpu.VMEM((2, half, H), F32),
        pltpu.VMEM((2, R, H), F32),
        pltpu.VMEM((2, R, H), F32),
        pltpu.VMEM((2, 4, R, H), BF16),
        pltpu.VMEM((2, NY, R, H), BF16),
        pltpu.VMEM((2, 4, R, H), BF16),
        pltpu.VMEM((2, NY, R, H), BF16),
        pltpu.VMEM((NY, R, H), F32),
        pltpu.VMEM((2, half, H), F32),
        pltpu.VMEM((3, 2, R, H), F32),
        pltpu.VMEM((3, 2, R, H), F32),
        pltpu.VMEM((NE, R, H), BF16),
        pltpu.VMEM((NE, R, H), BF16),
        pltpu.VMEM((NG, R, D), BF16),
    ]
    dma = pltpu.SemaphoreType.DMA
    return pl.pallas_call(
        merge_kernel,
        out_shape=(
            jax.ShapeDtypeStruct((TILE, D), BF16),
            jax.ShapeDtypeStruct((1, NG, TILE, D), BF16),
        ),
        in_specs=[hbm, smem, smem, smem, vmem, vmem],
        out_specs=(vmem, hbm),
        scratch_shapes=[
            pltpu.VMEM((TILE, D), F32),
            dma((2 * CHUNKS,)),
            dma((CHUNKS, NG)),
            dma((CHUNKS, NG)),
            dma((CHUNKS, 2, 6, 2)),
            dma((CHUNKS, 2, 6, 2)),
            dma((CHUNKS, 2, 6, 2)),
            dma((CHUNKS, 2, 6, 2)),
            dma((CHUNKS, NG)),
            dma((CHUNKS, NG)),
        ]
        + per_chunk * CHUNKS,
        compiler_params=pltpu.CompilerParams(
            collective_id=1, has_side_effects=True, vmem_limit_bytes=32 * MB
        ),
        name="merge_mirrors",
    )(part, prev, last, tid, grad_out, w_self)


def per_device(
    grad_out,
    in_degree,
    w_self,
    w_neigh,
    block_dst_tile,
    block_src_group,
    edge_dst,
    edge_src,
    block_count,
    mirror_tiles,
):
    ma, mb, counts, ids = gather(
        grad_out, in_degree.reshape(1, -1), w_neigh, edge_src, edge_dst, mirror_tiles
    )
    part, prev, last, tid = edge_sums(
        block_dst_tile, block_src_group, block_count, ids, counts, ma, mb
    )
    return merge(part, prev, last, tid, grad_out, w_self)


def solution(mesh):
    placed = (
        P(("grp", "edge"), None),
        P(("grp", "edge")),
        P(),
        P(),
        P(("grp", "edge")),
        P(("grp", "edge")),
        P(("grp", "edge"), None),
        P(("grp", "edge"), None),
        P(("grp", "edge")),
        P(("grp", "edge"), None),
    )
    return jax.shard_map(
        per_device,
        mesh=mesh,
        in_specs=placed,
        out_specs=(P(("grp", "edge"), None), P(("grp", "edge"), None, None, None)),
        check_vma=False,
    )
```

```python
import functools

import jax
import jax.numpy as jnp
from jax import lax
from jax.experimental import pallas as pl
from jax.experimental.pallas import tpu as pltpu
from jax.sharding import PartitionSpec as P

MESH = pl.DeviceIdType.MESH
NX, NY = 4, 8
NE = NX * NY
NG = 16
TILE = 128
D = 256
H = 128
B = 256
CHUNKS = 4
R = TILE // CHUNKS
VMEM_LIMIT = 40 * 1024 * 1024
LAG = 1
F32 = jnp.float32
BF16 = jnp.bfloat16
NT = (((1,), (1,)), ((), ()))


def here():
    e = lax.axis_index("edge")
    return lax.div(e, NY), lax.rem(e, NY)


def wrap_x(x):
    return lax.rem(x + 2 * NX, NX)


def wrap_y(y):
    return lax.rem(y + 2 * NY, NY)


def node(x, y):
    return {"edge": wrap_x(x) * NY + wrap_y(y)}


def plane_peers():
    x, y = here()
    return [node(x + j, y) for j in (1, 2, 3)] + [node(x, y + j) for j in (1, -1, 2, -2)]


def greet():
    barrier = pltpu.get_barrier_semaphore()
    peers = plane_peers()
    for peer in peers:
        pl.semaphore_signal(barrier, inc=1, device_id=peer, device_id_type=MESH)
    me = lax.axis_index("grp")

    def signal(i, carry):
        pl.semaphore_signal(
            barrier, inc=1, device_id={"grp": lax.rem(me + i, NG)}, device_id_type=MESH
        )
        return carry

    lax.fori_loop(1, NG, signal, 0)
    pl.semaphore_wait(barrier, len(peers) + NG - 1)


def gather_copies(fa, fb, send, recv):
    x, y = here()
    rows = fa.shape[1]

    def along_x(ref):
        return [(ref, node(x + j, y)) for j in (1, 2, 3)]

    def near_y(ref):
        return [(ref, node(x, y + j)) for j in (1, -1, 2, -2)]

    def group_a(yy):
        return wrap_y(yy) * NX

    def group_b(yy):
        return x * NY + wrap_y(yy)

    def half_b(yy, d):
        return fb.at[pl.ds(group_b(yy), 1), pl.ds(d * (rows // 2), rows // 2)]

    plan = [
        [
            along_x(fa.at[pl.ds(y * NX + x, 1)]),
            near_y(fa.at[pl.ds(y * NX, NX)]),
            [
                (fa.at[pl.ds(group_a(y - 2), NX)], node(x, y + 1)),
                (fa.at[pl.ds(group_a(y + 2), NX)], node(x, y - 1)),
                (fa.at[pl.ds(group_a(y - 2) + NX // 2, NX // 2)], node(x, y + 2)),
                (fa.at[pl.ds(group_a(y + 2), NX // 2)], node(x, y - 2)),
            ],
        ],
        [
            near_y(fb.at[pl.ds(group_b(y), 1)]),
            [
                (fb.at[pl.ds(group_b(y - 2), 1)], node(x, y + 1)),
                (fb.at[pl.ds(group_b(y + 2), 1)], node(x, y - 1)),
                (half_b(y - 2, 1), node(x, y + 2)),
                (half_b(y + 2, 0), node(x, y - 2)),
            ],
            along_x(fb.at[pl.ds(x * NY, NY)]),
        ],
    ]
    out = []
    for color in range(2):
        n = 0
        steps = []
        for step in plan[color]:
            copies = []
            for ref, to in step:
                copies.append(
                    pltpu.make_async_remote_copy(
                        src_ref=ref,
                        dst_ref=ref,
                        send_sem=send.at[color, n],
                        recv_sem=recv.at[color, n],
                        device_id=to,
                        device_id_type=MESH,
                    )
                )
                n += 1
            steps.append(copies)
        out.append(steps)
    return out


def gather_step(copies, color, stage):
    if stage > 0:
        for c in copies[color][stage - 1]:
            c.wait_recv()
    if stage < 3:
        for c in copies[color][stage]:
            c.start()


def gather_stage(copies, stage):
    for color in (1, 0):
        gather_step(copies, color, stage)


def gather_finish(copies):
    for color in range(2):
        for row in copies[color]:
            for c in row:
                c.wait_send()


SLOTS = 384


def block_order(group, tile, live):
    spread = jnp.broadcast_to(group, (TILE, B))
    slot_id = lax.broadcasted_iota(jnp.int32, (TILE, B), 1)
    mine = (lax.broadcasted_iota(jnp.int32, (TILE, B), 0) == spread) & (slot_id < live)
    hot = mine.astype(F32)
    before = lax.broadcasted_iota(jnp.int32, (B, B), 0) < lax.broadcasted_iota(
        jnp.int32, (B, B), 1
    )
    rank = jnp.dot(hot.astype(BF16), before.astype(F32).astype(BF16), preferred_element_type=F32)
    count = jnp.sum(hot, axis=1, keepdims=True).astype(jnp.int32)
    pairs = (count + 1) >> 1
    lower = lax.broadcasted_iota(jnp.int32, (TILE, TILE), 1) < lax.broadcasted_iota(
        jnp.int32, (TILE, TILE), 0
    )
    pairs_f = jnp.broadcast_to(pairs.astype(F32), (TILE, TILE))
    first = jnp.dot(
        lower.astype(F32).astype(BF16), pairs_f.astype(BF16), preferred_element_type=F32
    )
    place = 2.0 * first[:, 0:1] + rank + 1.0
    place = jnp.sum(hot * place, axis=0, keepdims=True).astype(jnp.int32) - 1
    hit = lax.broadcasted_iota(jnp.int32, (SLOTS, B), 0) == place
    row = lax.broadcasted_iota(jnp.int32, (8, B), 0)
    lane = lax.broadcasted_iota(jnp.int32, (8, B), 1)
    facts = jnp.where(row == 0, lane - B, jnp.where(row == 1, tile, group))
    found = lax.dot_general(
        facts.astype(F32).astype(BF16),
        hit.astype(F32).astype(BF16),
        NT,
        preferred_element_type=F32,
    ).astype(jnp.int32)
    row = lax.broadcasted_iota(jnp.int32, (8, SLOTS), 0)
    total = jnp.sum(pairs, axis=0, keepdims=True)
    return jnp.where(row == 0, found + B, jnp.where(row == 3, total, found))


def gather_kernel(
    g_any, deg_any, w_any, es_any, ed_any, mt_any, sg_any, dt_any, live_any,
    ma_ref, mb_ref, counts_ref, ids_ref, order_ref,
    g_ref, deg_ref, w_ref, es_ref, ed_ref, mt_ref, sg_ref, dt_ref, live_ref,
    in_sem, send, recv, id_send, id_recv,
):
    x, y = here()
    me = lax.axis_index("grp")
    pairs = (
        (g_any, g_ref), (w_any, w_ref), (deg_any, deg_ref), (mt_any, mt_ref), (sg_any, sg_ref),
        (dt_any, dt_ref), (live_any, live_ref), (es_any, es_ref), (ed_any, ed_ref),
    )
    loads = [
        pltpu.make_async_copy(src, dst, in_sem.at[i]) for i, (src, dst) in enumerate(pairs)
    ]
    for c in loads:
        c.start()
    for c in loads[:4]:
        c.wait()
    ids_ref[pl.ds(me, 1)] = jnp.zeros((1, 8, 128), jnp.int32)
    ids_ref[pl.ds(me, 1), 0:1, 0:NG] = mt_ref[...].reshape(1, 1, NG)
    neigh = lax.dot_general(g_ref[...], w_ref[...], NT, preferred_element_type=F32)
    deg = jnp.broadcast_to(deg_ref[...].astype(F32), (TILE, TILE)).T
    ma_ref[pl.ds(y * NX + x, 1)] = (neigh[:, :H] / deg).astype(BF16)[None]
    mb_ref[pl.ds(x * NY + y, 1)] = (neigh[:, H:] / deg).astype(BF16)[None]
    greet()

    copies = gather_copies(ma_ref, mb_ref, send, recv)
    rows_id = lax.broadcasted_iota(jnp.int32, (TILE, TILE), 0)

    def id_copy(i):
        peer = lax.rem(me + i, NG)
        return pltpu.make_async_remote_copy(
            src_ref=ids_ref.at[pl.ds(me, 1)],
            dst_ref=ids_ref.at[pl.ds(me, 1)],
            send_sem=id_send.at[i],
            recv_sem=id_recv.at[i],
            device_id={"grp": peer},
            device_id_type=MESH,
        )

    def one(b):
        src = (rows_id == es_ref[pl.ds(b, 1), :]).astype(F32).astype(BF16)
        dst = (rows_id == ed_ref[pl.ds(b, 1), :]).astype(F32).astype(BF16)
        counts_ref[pl.ds(b, 1)] = lax.dot_general(
            src, dst, NT, preferred_element_type=F32
        ).astype(BF16)[None]

    per_part = B // 8

    def build(first_part, parts):
        def body(i, carry):
            b = first_part * per_part + i * 8
            for j in range(8):
                one(b + j)
            return carry

        lax.fori_loop(0, parts * per_part // 8, body, 0)

    gather_stage(copies, 0)

    def start_id(i, carry):
        id_copy(i).start()
        return carry

    lax.fori_loop(1, NG, start_id, 0)
    for c in loads[4:]:
        c.wait()
    order_ref[...] = block_order(sg_ref[...], dt_ref[...], live_ref[...])
    counts_ref[B] = jnp.zeros((TILE, TILE), BF16)
    gather_step(copies, 0, 1)
    gather_step(copies, 1, 1)
    build(0, 1)
    gather_step(copies, 1, 2)
    build(1, 3)
    gather_step(copies, 0, 2)
    build(4, 4)
    gather_stage(copies, 3)

    def end_id(i, carry):
        id_copy(i).wait()
        return carry

    lax.fori_loop(1, NG, end_id, 0)
    gather_finish(copies)


def gather(grad_out, deg, w_neigh, edge_src, edge_dst, mirror_tiles, group, tile, live):
    vmem = pl.BlockSpec(memory_space=pltpu.VMEM)
    ins = (grad_out, deg, w_neigh, edge_src, edge_dst, mirror_tiles, group, tile, live)
    return pl.pallas_call(
        gather_kernel,
        out_shape=(
            jax.ShapeDtypeStruct((NE, TILE, H), BF16),
            jax.ShapeDtypeStruct((NE, TILE, H), BF16),
            jax.ShapeDtypeStruct((B + 1, TILE, TILE), BF16),
            jax.ShapeDtypeStruct((NG, 8, 128), jnp.int32),
            jax.ShapeDtypeStruct((8, SLOTS), jnp.int32),
        ),
        in_specs=[pl.BlockSpec(memory_space=pltpu.HBM)] * len(ins),
        out_specs=(vmem,) * 5,
        scratch_shapes=[pltpu.VMEM(v.shape, v.dtype) for v in ins]
        + [
            pltpu.SemaphoreType.DMA((len(ins),)),
            pltpu.SemaphoreType.DMA((2, 11)),
            pltpu.SemaphoreType.DMA((2, 11)),
            pltpu.SemaphoreType.DMA((NG,)),
            pltpu.SemaphoreType.DMA((NG,)),
        ],
        compiler_params=pltpu.CompilerParams(
            collective_id=0, has_side_effects=True, vmem_limit_bytes=VMEM_LIMIT
        ),
        name="gather_messages",
    )(*ins)


UNROLL = 4


def sum_kernel(
    order_ref, ids_ref, counts_ref, ma_ref, mb_ref,
    part_ref, prev_ref, last_ref, tid_ref,
    sums,
):
    me = lax.axis_index("grp")

    def clear(t, carry):
        last_ref[t] = NG
        return carry

    lax.fori_loop(0, NE, clear, 0)

    def link(g, carry):
        t = ids_ref[g, 0, me]
        tid_ref[g] = t
        prev_ref[g] = last_ref[t]
        last_ref[t] = g
        return carry

    lax.fori_loop(0, NG, link, 0)
    sums[...] = jnp.zeros_like(sums)

    def tile_of(t):
        ia = lax.rem(t, NY) * NX + lax.div(t, NY)
        return jnp.concatenate([ma_ref[ia], mb_ref[t]], axis=1)

    def turn(i, carry):
        for j in range(UNROLL):
            p = 2 * (i * UNROLL + j)
            lhs = jnp.concatenate(
                [counts_ref[order_ref[0, p]], counts_ref[order_ref[0, p + 1]]], axis=1
            )
            rhs = jnp.concatenate(
                [tile_of(order_ref[1, p]), tile_of(order_ref[1, p + 1])], axis=0
            )
            s = order_ref[2, p]
            sums[s] = sums[s] + jnp.dot(lhs, rhs, preferred_element_type=F32)
        return carry

    lax.fori_loop(0, lax.div(order_ref[3, 0] + UNROLL - 1, UNROLL), turn, 0)

    def write(s, carry):
        for c in range(CHUNKS):
            for h in range(2):
                part_ref[c, s, h] = sums[s, c * R : (c + 1) * R, h * H : (h + 1) * H].astype(BF16)
        return carry

    lax.fori_loop(0, NG, write, 0)


def edge_sums(order, ids, counts, ma, mb):
    smem = pl.BlockSpec(memory_space=pltpu.SMEM)
    vmem = pl.BlockSpec(memory_space=pltpu.VMEM)
    return pl.pallas_call(
        sum_kernel,
        out_shape=(
            jax.ShapeDtypeStruct((CHUNKS, NG, 2, R, H), BF16),
            jax.ShapeDtypeStruct((NG,), jnp.int32),
            jax.ShapeDtypeStruct((NE,), jnp.int32),
            jax.ShapeDtypeStruct((NG,), jnp.int32),
        ),
        in_specs=[smem, smem, vmem, vmem, vmem],
        out_specs=(vmem, smem, smem, smem),
        scratch_shapes=[pltpu.VMEM((NG, TILE, D), F32)],
        compiler_params=pltpu.CompilerParams(vmem_limit_bytes=VMEM_LIMIT),
        name="edge_sums",
    )(order, ids, counts, ma, mb)


NAMES = (
    "relay", "sums", "ua", "ub", "fa", "fb", "picked",
    "sfara", "sneara", "shalfa", "smida", "sxa", "sfarb", "snearb", "shalfb", "smidb", "sxb",
    "rfara", "rneara", "rhalfa", "rmida", "rxa", "rfarb", "rnearb", "rhalfb", "rmidb", "rxb",
)
Z_ORDER = (8, 9, 7, 6, 10, 5, 11, 4, 12, 3, 13, 2, 14, 1, 15)


def merge_kernel(
    part_ref, prev_ref, last_ref, tid_ref, g_any, w_any,
    gf_ref, mg_ref,
    g_ref, w_ref, in_sem,
    self_term, own_sem, z_send, z_recv, r_send, r_recv, f_send, f_recv, b_send, b_recv,
    *bufs,
):
    x, y = here()
    me = lax.axis_index("grp")
    chunks = [dict(zip(NAMES, bufs[c * len(NAMES) : (c + 1) * len(NAMES)])) for c in range(CHUNKS)]
    loads = [
        pltpu.make_async_copy(g_any, g_ref, in_sem.at[0]),
        pltpu.make_async_copy(w_any, w_ref, in_sem.at[1]),
    ]
    for c in loads:
        c.start()

    greet()

    def z_copy(c, i):
        peer = lax.rem(me + i, NG)
        return pltpu.make_async_remote_copy(
            src_ref=part_ref.at[c, peer],
            dst_ref=chunks[c]["relay"].at[me],
            send_sem=z_send.at[c, i],
            recv_sem=z_recv.at[c, i],
            device_id={"grp": peer},
            device_id_type=MESH,
        )

    def own_copy(c):
        return pltpu.make_async_copy(
            part_ref.at[c, me], chunks[c]["relay"].at[me], own_sem.at[c]
        )

    for c in range(CHUNKS):
        own_copy(c).start()
        for i in Z_ORDER:
            z_copy(c, i).start()

    for c in loads:
        c.wait()
    self_term[...] = lax.dot_general(g_ref[...], w_ref[...], NT, preferred_element_type=F32)

    y_hop = (1, -1, 1, -1, 2, -2, 2, -2)

    def ring_copy(c, color, n):
        buf = chunks[c]
        kind = ("far", "near", "half", "mid")[n // 2] if n < 8 else "x"
        d = n % 2 if n < 8 else n - 8
        to = node(x, y + y_hop[n]) if n < 8 else node(x + d + 1, y)
        name = kind + "ab"[color]
        return pltpu.make_async_remote_copy(
            src_ref=buf["s" + name].at[d],
            dst_ref=buf["r" + name].at[d],
            send_sem=r_send.at[c, color, n],
            recv_sem=r_recv.at[c, color, n],
            device_id=to,
            device_id_type=MESH,
        )

    def start(c, color, which):
        for n in which:
            ring_copy(c, color, n).start()

    def arrived(c, color, which):
        for n in which:
            ring_copy(c, color, n).wait_recv()

    first, second, cross = (0, 1, 2, 3, 4, 5), (6, 7), (8, 9, 10)

    def tile_sum(c, color, xx, yy):
        return chunks[c]["sums"][last_ref[xx * NY + yy], color]

    def relay_stage(c):
        buf = chunks[c]
        own_copy(c).wait()

        def arrive(i, carry):
            z_copy(c, i).wait_recv()
            return carry

        lax.fori_loop(1, NG, arrive, 0)
        buf["sums"][NG] = jnp.zeros((2, R, H), F32)
        for g in range(NG):
            buf["sums"][g] = buf["relay"][g].astype(F32) + buf["sums"][prev_ref[g]]

    half_rows = R // 2

    def reduce_a(c, k):
        buf = chunks[c]
        if k == 0:
            for d in range(2):
                sign = 1 - 2 * d
                for xx in range(NX):
                    buf["sfara"][d, xx] = tile_sum(c, 0, xx, wrap_y(y + 3 * sign)).astype(BF16)
                    buf["sneara"][d, xx] = tile_sum(c, 0, xx, wrap_y(y + sign)).astype(BF16)
                for j in range(2):
                    buf["shalfa"][d, j] = tile_sum(c, 0, 2 * d + j, wrap_y(y + 4)).astype(BF16)
            start(c, 0, first)
        elif k == 1:
            arrived(c, 0, first)
            for d in range(2):
                yy = wrap_y(y + 2 * (1 - 2 * d))
                for xx in range(NX):
                    v = tile_sum(c, 0, xx, yy) + buf["rfara"][d, xx].astype(F32)
                    if xx // 2 == d:
                        v = v + buf["rhalfa"][d, xx % 2].astype(F32)
                    buf["smida"][d, xx] = v.astype(BF16)
            start(c, 0, second)
        elif k == 2:
            arrived(c, 0, second)
            for xx in range(NX):
                v = tile_sum(c, 0, xx, y)
                for d in range(2):
                    v = v + buf["rneara"][d, xx].astype(F32) + buf["rmida"][d, xx].astype(F32)
                buf["ua"][xx] = v
            for j in range(3):
                buf["sxa"][j] = buf["ua"][wrap_x(x + j + 1)].astype(BF16)
            start(c, 0, cross)
        else:
            arrived(c, 0, cross)
            v = buf["ua"][x]
            for j in range(3):
                v = v + buf["rxa"][j].astype(F32)
            return v

    def reduce_b(c, k):
        buf = chunks[c]
        if k == 0:
            for j in range(3):
                xx = wrap_x(x + j + 1)
                for yy in range(NY):
                    buf["sxb"][j, yy] = tile_sum(c, 1, xx, yy).astype(BF16)
            start(c, 1, cross)
        elif k == 1:
            arrived(c, 1, cross)
            for yy in range(NY):
                v = tile_sum(c, 1, x, yy)
                for j in range(3):
                    v = v + buf["rxb"][j, yy].astype(F32)
                buf["ub"][yy] = v
            for d in range(2):
                sign = 1 - 2 * d
                buf["sfarb"][d] = buf["ub"][wrap_y(y + 3 * sign)].astype(BF16)
                buf["snearb"][d] = buf["ub"][wrap_y(y + sign)].astype(BF16)
                half = pl.ds(d * half_rows, half_rows)
                buf["shalfb"][d] = buf["ub"][wrap_y(y + 4), half].astype(BF16)
            start(c, 1, first)
        elif k == 2:
            arrived(c, 1, first)
            for d in range(2):
                v = buf["ub"][wrap_y(y + 2 * (1 - 2 * d))] + buf["rfarb"][d].astype(F32)
                parts = [v[:half_rows], v[half_rows:]]
                parts[d] = parts[d] + buf["rhalfb"][d].astype(F32)
                for j in range(2):
                    buf["smidb"][d, j * half_rows : (j + 1) * half_rows] = parts[j].astype(BF16)
            start(c, 1, second)
        else:
            arrived(c, 1, second)
            v = buf["ub"][y]
            for d in range(2):
                v = v + buf["rnearb"][d].astype(F32) + buf["rmidb"][d].astype(F32)
            return v

    gathers = [
        gather_copies(chunks[c]["fa"], chunks[c]["fb"], f_send.at[c], f_recv.at[c])
        for c in range(CHUNKS)
    ]

    def back_copy(c, i):
        peer = lax.rem(me + i, NG)
        return pltpu.make_async_remote_copy(
            src_ref=chunks[c]["picked"].at[peer],
            dst_ref=mg_ref.at[0, me, pl.ds(c * R, R)],
            send_sem=b_send.at[c, i],
            recv_sem=b_recv.at[c, i],
            device_id={"grp": peer},
            device_id_type=MESH,
        )

    def back_own(c):
        return pltpu.make_async_copy(
            chunks[c]["picked"].at[me], mg_ref.at[0, me, pl.ds(c * R, R)], own_sem.at[CHUNKS + c]
        )

    def finish_tile(c):
        buf = chunks[c]
        own_a = reduce_a(c, 3)
        own_b = reduce_b(c, 3)
        rows = pl.ds(c * R, R)
        out_a = (self_term[rows, 0:H] + own_a).astype(BF16)
        out_b = (self_term[rows, H:D] + own_b).astype(BF16)
        gf_ref[rows, 0:H] = out_a
        gf_ref[rows, H:D] = out_b
        buf["fa"][pl.ds(y * NX + x, 1)] = out_a[None]
        buf["fb"][pl.ds(x * NY + y, 1)] = out_b[None]
        gather_stage(gathers[c], 0)

    def send_back(c):
        buf = chunks[c]
        gather_stage(gathers[c], 3)
        for g in range(NG):
            t = tid_ref[g]
            ia = lax.rem(t, NY) * NX + lax.div(t, NY)
            buf["picked"][g, :, 0:H] = buf["fa"][ia]
            buf["picked"][g, :, H:D] = buf["fb"][t]
        back_own(c).start()
        for i in Z_ORDER:
            back_copy(c, i).start()

    stages = []
    for k in range(3):
        def reduce_step(c, k=k):
            if k == 0:
                relay_stage(c)
            reduce_a(c, k)
            reduce_b(c, k)
        stages.append(reduce_step)
    stages.append(finish_tile)
    for k in range(1, 3):
        stages.append(lambda c, k=k: gather_stage(gathers[c], k))
    stages.append(send_back)

    lag = LAG
    for tick in range(len(stages) + lag * (CHUNKS - 1)):
        for c in range(CHUNKS):
            k = tick - lag * c
            if 0 <= k < len(stages):
                stages[k](c)

    for c in range(CHUNKS):
        back_own(c).wait()

        def end(i, carry, c=c):
            z_copy(c, i).wait_send()
            back_copy(c, i).wait()
            return carry

        lax.fori_loop(1, NG, end, 0)
        for color in range(2):
            for n in range(11):
                ring_copy(c, color, n).wait_send()
        gather_finish(gathers[c])


def merge(part, prev, last, tid, grad_out, w_self):
    smem = pl.BlockSpec(memory_space=pltpu.SMEM)
    vmem = pl.BlockSpec(memory_space=pltpu.VMEM)
    hbm = pl.BlockSpec(memory_space=pl.ANY)
    kept = pl.BlockSpec(memory_space=pltpu.HBM)
    half = R // 2
    shapes = dict(
        relay=((NG, 2, R, H), BF16),
        sums=((NG + 1, 2, R, H), F32),
        ua=((NX, R, H), F32),
        ub=((NY, R, H), F32),
        fa=((NE, R, H), BF16),
        fb=((NE, R, H), BF16),
        picked=((NG, R, D), BF16),
    )
    for side in "sr":
        shapes[side + "fara"] = ((2, NX, R, H), BF16)
        shapes[side + "neara"] = ((2, NX, R, H), BF16)
        shapes[side + "halfa"] = ((2, NX // 2, R, H), BF16)
        shapes[side + "mida"] = ((2, NX, R, H), BF16)
        shapes[side + "xa"] = ((3, R, H), BF16)
        shapes[side + "farb"] = ((2, R, H), BF16)
        shapes[side + "nearb"] = ((2, R, H), BF16)
        shapes[side + "halfb"] = ((2, half, H), BF16)
        shapes[side + "midb"] = ((2, R, H), BF16)
        shapes[side + "xb"] = ((3, NY, R, H), BF16)
    per_chunk = [pltpu.VMEM(*shapes[name]) for name in NAMES]
    dma = pltpu.SemaphoreType.DMA
    return pl.pallas_call(
        merge_kernel,
        out_shape=(
            jax.ShapeDtypeStruct((TILE, D), BF16),
            jax.ShapeDtypeStruct((1, NG, TILE, D), BF16),
        ),
        in_specs=[hbm, smem, smem, smem, kept, kept],
        out_specs=(vmem, hbm),
        scratch_shapes=[
            pltpu.VMEM((TILE, D), BF16),
            pltpu.VMEM((D, D), BF16),
            dma((2,)),
            pltpu.VMEM((TILE, D), F32),
            dma((2 * CHUNKS,)),
            dma((CHUNKS, NG)),
            dma((CHUNKS, NG)),
            dma((CHUNKS, 2, 11)),
            dma((CHUNKS, 2, 11)),
            dma((CHUNKS, 2, 11)),
            dma((CHUNKS, 2, 11)),
            dma((CHUNKS, NG)),
            dma((CHUNKS, NG)),
        ]
        + per_chunk * CHUNKS,
        compiler_params=pltpu.CompilerParams(
            collective_id=1, has_side_effects=True, vmem_limit_bytes=VMEM_LIMIT
        ),
        name="merge_mirrors",
    )(part, prev, last, tid, grad_out, w_self)


def per_device(
    grad_out,
    in_degree,
    w_self,
    w_neigh,
    block_dst_tile,
    block_src_group,
    edge_dst,
    edge_src,
    block_count,
    mirror_tiles,
):
    ma, mb, counts, ids, order = gather(
        grad_out,
        in_degree.reshape(1, -1),
        w_neigh,
        edge_src,
        edge_dst,
        mirror_tiles,
        block_src_group.reshape(1, -1),
        block_dst_tile.reshape(1, -1),
        block_count.reshape(1, 1),
    )
    part, prev, last, tid = edge_sums(order, ids, counts, ma, mb)
    return merge(part, prev, last, tid, grad_out, w_self)


def solution(mesh):
    placed = (
        P(("grp", "edge"), None),
        P(("grp", "edge")),
        P(),
        P(),
        P(("grp", "edge")),
        P(("grp", "edge")),
        P(("grp", "edge"), None),
        P(("grp", "edge"), None),
        P(("grp", "edge")),
        P(("grp", "edge"), None),
    )
    return jax.shard_map(
        per_device,
        mesh=mesh,
        in_specs=placed,
        out_specs=(P(("grp", "edge"), None), P(("grp", "edge"), None, None, None)),
        check_vma=False,
    )
```

```python
import functools

import jax
import jax.numpy as jnp
from jax import lax
from jax.experimental import pallas as pl
from jax.experimental.pallas import tpu as pltpu
from jax.sharding import PartitionSpec as P

MESH = pl.DeviceIdType.MESH
NX, NY = 4, 8
NE = NX * NY
NG = 16
TILE = 128
D = 256
H = 128
B = 256
CHUNKS = 4
R = TILE // CHUNKS
VMEM_LIMIT = 40 * 1024 * 1024
LAG = 1
F32 = jnp.float32
BF16 = jnp.bfloat16
NT = (((1,), (1,)), ((), ()))


def here():
    e = lax.axis_index("edge")
    return lax.div(e, NY), lax.rem(e, NY)


def wrap_x(x):
    return lax.rem(x + 2 * NX, NX)


def wrap_y(y):
    return lax.rem(y + 2 * NY, NY)


def node(x, y):
    return {"edge": wrap_x(x) * NY + wrap_y(y)}


def plane_peers():
    x, y = here()
    return [node(x + j, y) for j in (1, 2, 3)] + [node(x, y + j) for j in (1, -1, 2, -2)]


def greet():
    barrier = pltpu.get_barrier_semaphore()
    peers = plane_peers()
    for peer in peers:
        pl.semaphore_signal(barrier, inc=1, device_id=peer, device_id_type=MESH)
    me = lax.axis_index("grp")

    def signal(i, carry):
        pl.semaphore_signal(
            barrier, inc=1, device_id={"grp": lax.rem(me + i, NG)}, device_id_type=MESH
        )
        return carry

    lax.fori_loop(1, NG, signal, 0)
    pl.semaphore_wait(barrier, len(peers) + NG - 1)


def gather_copies(fa, fb, send, recv):
    x, y = here()
    rows = fa.shape[1]

    def along_x(ref):
        return [(ref, node(x + j, y)) for j in (1, 2, 3)]

    def near_y(ref):
        return [(ref, node(x, y + j)) for j in (1, -1, 2, -2)]

    def group_a(yy):
        return wrap_y(yy) * NX

    def group_b(yy):
        return x * NY + wrap_y(yy)

    def half_b(yy, d):
        return fb.at[pl.ds(group_b(yy), 1), pl.ds(d * (rows // 2), rows // 2)]

    plan = [
        [
            along_x(fa.at[pl.ds(y * NX + x, 1)]),
            near_y(fa.at[pl.ds(y * NX, NX)]),
            [
                (fa.at[pl.ds(group_a(y - 2), NX)], node(x, y + 1)),
                (fa.at[pl.ds(group_a(y + 2), NX)], node(x, y - 1)),
                (fa.at[pl.ds(group_a(y - 2) + NX // 2, NX // 2)], node(x, y + 2)),
                (fa.at[pl.ds(group_a(y + 2), NX // 2)], node(x, y - 2)),
            ],
        ],
        [
            near_y(fb.at[pl.ds(group_b(y), 1)]),
            [
                (fb.at[pl.ds(group_b(y - 2), 1)], node(x, y + 1)),
                (fb.at[pl.ds(group_b(y + 2), 1)], node(x, y - 1)),
                (half_b(y - 2, 1), node(x, y + 2)),
                (half_b(y + 2, 0), node(x, y - 2)),
            ],
            along_x(fb.at[pl.ds(x * NY, NY)]),
        ],
    ]
    out = []
    for color in range(2):
        n = 0
        steps = []
        for step in plan[color]:
            copies = []
            for ref, to in step:
                copies.append(
                    pltpu.make_async_remote_copy(
                        src_ref=ref,
                        dst_ref=ref,
                        send_sem=send.at[color, n],
                        recv_sem=recv.at[color, n],
                        device_id=to,
                        device_id_type=MESH,
                    )
                )
                n += 1
            steps.append(copies)
        out.append(steps)
    return out


def gather_step(copies, color, stage):
    if stage > 0:
        for c in copies[color][stage - 1]:
            c.wait_recv()
    if stage < 3:
        for c in copies[color][stage]:
            c.start()


def gather_stage(copies, stage):
    for color in (1, 0):
        gather_step(copies, color, stage)


def gather_finish(copies):
    for color in range(2):
        for row in copies[color]:
            for c in row:
                c.wait_send()


SLOTS = 384


def block_order(group, tile, live):
    spread = jnp.broadcast_to(group, (TILE, B))
    slot_id = lax.broadcasted_iota(jnp.int32, (TILE, B), 1)
    mine = (lax.broadcasted_iota(jnp.int32, (TILE, B), 0) == spread) & (slot_id < live)
    hot = mine.astype(F32)
    before = lax.broadcasted_iota(jnp.int32, (B, B), 0) < lax.broadcasted_iota(
        jnp.int32, (B, B), 1
    )
    rank = jnp.dot(hot.astype(BF16), before.astype(F32).astype(BF16), preferred_element_type=F32)
    count = jnp.sum(hot, axis=1, keepdims=True).astype(jnp.int32)
    pairs = (count + 1) >> 1
    lower = lax.broadcasted_iota(jnp.int32, (TILE, TILE), 1) < lax.broadcasted_iota(
        jnp.int32, (TILE, TILE), 0
    )
    pairs_f = jnp.broadcast_to(pairs.astype(F32), (TILE, TILE))
    first = jnp.dot(
        lower.astype(F32).astype(BF16), pairs_f.astype(BF16), preferred_element_type=F32
    )
    place = 2.0 * first[:, 0:1] + rank + 1.0
    place = jnp.sum(hot * place, axis=0, keepdims=True).astype(jnp.int32) - 1
    hit = lax.broadcasted_iota(jnp.int32, (SLOTS, B), 0) == place
    row = lax.broadcasted_iota(jnp.int32, (8, B), 0)
    lane = lax.broadcasted_iota(jnp.int32, (8, B), 1)
    facts = jnp.where(row == 0, lane - B, jnp.where(row == 1, tile, group))
    found = lax.dot_general(
        facts.astype(F32).astype(BF16),
        hit.astype(F32).astype(BF16),
        NT,
        preferred_element_type=F32,
    ).astype(jnp.int32)
    row = lax.broadcasted_iota(jnp.int32, (8, SLOTS), 0)
    total = jnp.sum(pairs, axis=0, keepdims=True)
    return jnp.where(row == 0, found + B, jnp.where(row == 3, total, found))


def gather_kernel(
    g_any, deg_any, w_any, es_any, ed_any, mt_any, sg_any, dt_any, live_any,
    ma_ref, mb_ref, counts_ref, ids_ref, order_ref,
    g_ref, deg_ref, w_ref, es_ref, ed_ref, mt_ref, sg_ref, dt_ref, live_ref,
    in_sem, send, recv, id_send, id_recv,
):
    x, y = here()
    me = lax.axis_index("grp")
    pairs = (
        (g_any, g_ref), (w_any, w_ref), (deg_any, deg_ref), (mt_any, mt_ref), (sg_any, sg_ref),
        (dt_any, dt_ref), (live_any, live_ref), (es_any, es_ref), (ed_any, ed_ref),
    )
    loads = [
        pltpu.make_async_copy(src, dst, in_sem.at[i]) for i, (src, dst) in enumerate(pairs)
    ]
    for c in loads:
        c.start()
    for c in loads[:4]:
        c.wait()
    ids_ref[pl.ds(me, 1)] = jnp.zeros((1, 8, 128), jnp.int32)
    ids_ref[pl.ds(me, 1), 0:1, 0:NG] = mt_ref[...].reshape(1, 1, NG)
    neigh = lax.dot_general(g_ref[...], w_ref[...], NT, preferred_element_type=F32)
    deg = jnp.broadcast_to(deg_ref[...].astype(F32), (TILE, TILE)).T
    ma_ref[pl.ds(y * NX + x, 1)] = (neigh[:, :H] / deg).astype(BF16)[None]
    mb_ref[pl.ds(x * NY + y, 1)] = (neigh[:, H:] / deg).astype(BF16)[None]
    greet()

    copies = gather_copies(ma_ref, mb_ref, send, recv)
    rows_id = lax.broadcasted_iota(jnp.int32, (TILE, TILE), 0)

    def id_copy(i):
        peer = lax.rem(me + i, NG)
        return pltpu.make_async_remote_copy(
            src_ref=ids_ref.at[pl.ds(me, 1)],
            dst_ref=ids_ref.at[pl.ds(me, 1)],
            send_sem=id_send.at[i],
            recv_sem=id_recv.at[i],
            device_id={"grp": peer},
            device_id_type=MESH,
        )

    def one(b):
        src = (rows_id == es_ref[pl.ds(b, 1), :]).astype(F32).astype(BF16)
        dst = (rows_id == ed_ref[pl.ds(b, 1), :]).astype(F32).astype(BF16)
        counts_ref[pl.ds(b, 1)] = lax.dot_general(
            src, dst, NT, preferred_element_type=F32
        ).astype(BF16)[None]

    per_part = B // 8

    def build(first_part, parts):
        def body(i, carry):
            b = first_part * per_part + i * 8
            for j in range(8):
                one(b + j)
            return carry

        lax.fori_loop(0, parts * per_part // 8, body, 0)

    gather_stage(copies, 0)

    def start_id(i, carry):
        id_copy(i).start()
        return carry

    lax.fori_loop(1, NG, start_id, 0)
    for c in loads[4:]:
        c.wait()
    order_ref[...] = block_order(sg_ref[...], dt_ref[...], live_ref[...])
    counts_ref[B] = jnp.zeros((TILE, TILE), BF16)
    gather_step(copies, 0, 1)
    gather_step(copies, 1, 1)
    build(0, 1)
    gather_step(copies, 1, 2)
    build(1, 3)
    gather_step(copies, 0, 2)
    build(4, 4)
    gather_stage(copies, 3)

    def end_id(i, carry):
        id_copy(i).wait()
        return carry

    lax.fori_loop(1, NG, end_id, 0)
    gather_finish(copies)


def gather(grad_out, deg, w_neigh, edge_src, edge_dst, mirror_tiles, group, tile, live):
    vmem = pl.BlockSpec(memory_space=pltpu.VMEM)
    ins = (grad_out, deg, w_neigh, edge_src, edge_dst, mirror_tiles, group, tile, live)
    return pl.pallas_call(
        gather_kernel,
        out_shape=(
            jax.ShapeDtypeStruct((NE, TILE, H), BF16),
            jax.ShapeDtypeStruct((NE, TILE, H), BF16),
            jax.ShapeDtypeStruct((B + 1, TILE, TILE), BF16),
            jax.ShapeDtypeStruct((NG, 8, 128), jnp.int32),
            jax.ShapeDtypeStruct((8, SLOTS), jnp.int32),
        ),
        in_specs=[pl.BlockSpec(memory_space=pltpu.HBM)] * len(ins),
        out_specs=(vmem,) * 5,
        scratch_shapes=[pltpu.VMEM(v.shape, v.dtype) for v in ins]
        + [
            pltpu.SemaphoreType.DMA((len(ins),)),
            pltpu.SemaphoreType.DMA((2, 11)),
            pltpu.SemaphoreType.DMA((2, 11)),
            pltpu.SemaphoreType.DMA((NG,)),
            pltpu.SemaphoreType.DMA((NG,)),
        ],
        compiler_params=pltpu.CompilerParams(
            collective_id=0, has_side_effects=True, vmem_limit_bytes=VMEM_LIMIT
        ),
        name="gather_messages",
    )(*[pltpu.with_memory_space_constraint(v, pltpu.HBM) for v in ins[:-1]], live)


UNROLL = 4


def sum_kernel(
    order_ref, ids_ref, counts_ref, ma_ref, mb_ref,
    part_ref, prev_ref, last_ref, tid_ref,
    sums,
):
    me = lax.axis_index("grp")

    def clear(t, carry):
        last_ref[t] = NG
        return carry

    lax.fori_loop(0, NE, clear, 0)

    def link(g, carry):
        t = ids_ref[g, 0, me]
        tid_ref[g] = t
        prev_ref[g] = last_ref[t]
        last_ref[t] = g
        return carry

    lax.fori_loop(0, NG, link, 0)
    sums[...] = jnp.zeros_like(sums)

    def tile_of(t):
        ia = lax.rem(t, NY) * NX + lax.div(t, NY)
        return jnp.concatenate([ma_ref[ia], mb_ref[t]], axis=1)

    def turn(i, carry):
        for j in range(UNROLL):
            p = 2 * (i * UNROLL + j)
            lhs = jnp.concatenate(
                [counts_ref[order_ref[0, p]], counts_ref[order_ref[0, p + 1]]], axis=1
            )
            rhs = jnp.concatenate(
                [tile_of(order_ref[1, p]), tile_of(order_ref[1, p + 1])], axis=0
            )
            s = order_ref[2, p]
            sums[s] = sums[s] + jnp.dot(lhs, rhs, preferred_element_type=F32)
        return carry

    lax.fori_loop(0, lax.div(order_ref[3, 0] + UNROLL - 1, UNROLL), turn, 0)

    def write(s, carry):
        for c in range(CHUNKS):
            for h in range(2):
                part_ref[c, s, h] = sums[s, c * R : (c + 1) * R, h * H : (h + 1) * H].astype(BF16)
        return carry

    lax.fori_loop(0, NG, write, 0)


def edge_sums(order, ids, counts, ma, mb):
    smem = pl.BlockSpec(memory_space=pltpu.SMEM)
    vmem = pl.BlockSpec(memory_space=pltpu.VMEM)
    return pl.pallas_call(
        sum_kernel,
        out_shape=(
            jax.ShapeDtypeStruct((CHUNKS, NG, 2, R, H), BF16),
            jax.ShapeDtypeStruct((NG,), jnp.int32),
            jax.ShapeDtypeStruct((NE,), jnp.int32),
            jax.ShapeDtypeStruct((NG,), jnp.int32),
        ),
        in_specs=[smem, smem, vmem, vmem, vmem],
        out_specs=(vmem, smem, smem, smem),
        scratch_shapes=[pltpu.VMEM((NG, TILE, D), F32)],
        compiler_params=pltpu.CompilerParams(vmem_limit_bytes=VMEM_LIMIT),
        name="edge_sums",
    )(order, ids, counts, ma, mb)


NAMES = (
    "relay", "sums", "ua", "ub", "fa", "fb", "picked",
    "sfara", "sneara", "shalfa", "smida", "sxa", "sfarb", "snearb", "shalfb", "smidb", "sxb",
    "rfara", "rneara", "rhalfa", "rmida", "rxa", "rfarb", "rnearb", "rhalfb", "rmidb", "rxb",
)
Z_ORDER = (8, 9, 7, 6, 10, 5, 11, 4, 12, 3, 13, 2, 14, 1, 15)


def merge_kernel(
    part_ref, prev_ref, last_ref, tid_ref, g_any, w_any,
    gf_ref, mg_ref,
    g_ref, w_ref, in_sem,
    self_term, own_sem, z_send, z_recv, r_send, r_recv, f_send, f_recv, b_send, b_recv,
    *bufs,
):
    x, y = here()
    me = lax.axis_index("grp")
    chunks = [dict(zip(NAMES, bufs[c * len(NAMES) : (c + 1) * len(NAMES)])) for c in range(CHUNKS)]
    loads = [
        pltpu.make_async_copy(g_any, g_ref, in_sem.at[0]),
        pltpu.make_async_copy(w_any, w_ref, in_sem.at[1]),
    ]
    for c in loads:
        c.start()

    greet()

    def z_copy(c, i):
        peer = lax.rem(me + i, NG)
        return pltpu.make_async_remote_copy(
            src_ref=part_ref.at[c, peer],
            dst_ref=chunks[c]["relay"].at[me],
            send_sem=z_send.at[c, i],
            recv_sem=z_recv.at[c, i],
            device_id={"grp": peer},
            device_id_type=MESH,
        )

    def own_copy(c):
        return pltpu.make_async_copy(
            part_ref.at[c, me], chunks[c]["relay"].at[me], own_sem.at[c]
        )

    for c in range(CHUNKS):
        own_copy(c).start()
        for i in Z_ORDER:
            z_copy(c, i).start()

    for c in loads:
        c.wait()
    self_term[...] = lax.dot_general(g_ref[...], w_ref[...], NT, preferred_element_type=F32)

    y_hop = (1, -1, 1, -1, 2, -2, 2, -2)

    def ring_copy(c, color, n):
        buf = chunks[c]
        kind = ("far", "near", "half", "mid")[n // 2] if n < 8 else "x"
        d = n % 2 if n < 8 else n - 8
        to = node(x, y + y_hop[n]) if n < 8 else node(x + d + 1, y)
        name = kind + "ab"[color]
        return pltpu.make_async_remote_copy(
            src_ref=buf["s" + name].at[d],
            dst_ref=buf["r" + name].at[d],
            send_sem=r_send.at[c, color, n],
            recv_sem=r_recv.at[c, color, n],
            device_id=to,
            device_id_type=MESH,
        )

    def start(c, color, which):
        for n in which:
            ring_copy(c, color, n).start()

    def arrived(c, color, which):
        for n in which:
            ring_copy(c, color, n).wait_recv()

    first, second, cross = (0, 1, 2, 3, 4, 5), (6, 7), (8, 9, 10)

    def tile_sum(c, color, xx, yy):
        return chunks[c]["sums"][last_ref[xx * NY + yy], color]

    def relay_stage(c):
        buf = chunks[c]
        own_copy(c).wait()

        def arrive(i, carry):
            z_copy(c, i).wait_recv()
            return carry

        lax.fori_loop(1, NG, arrive, 0)
        buf["sums"][NG] = jnp.zeros((2, R, H), F32)
        for g in range(NG):
            buf["sums"][g] = buf["relay"][g].astype(F32) + buf["sums"][prev_ref[g]]

    half_rows = R // 2

    def reduce_a(c, k):
        buf = chunks[c]
        if k == 0:
            for d in range(2):
                sign = 1 - 2 * d
                for xx in range(NX):
                    buf["sfara"][d, xx] = tile_sum(c, 0, xx, wrap_y(y + 3 * sign)).astype(BF16)
                    buf["sneara"][d, xx] = tile_sum(c, 0, xx, wrap_y(y + sign)).astype(BF16)
                for j in range(2):
                    buf["shalfa"][d, j] = tile_sum(c, 0, 2 * d + j, wrap_y(y + 4)).astype(BF16)
            start(c, 0, first)
        elif k == 1:
            arrived(c, 0, first)
            for d in range(2):
                yy = wrap_y(y + 2 * (1 - 2 * d))
                for xx in range(NX):
                    v = tile_sum(c, 0, xx, yy) + buf["rfara"][d, xx].astype(F32)
                    if xx // 2 == d:
                        v = v + buf["rhalfa"][d, xx % 2].astype(F32)
                    buf["smida"][d, xx] = v.astype(BF16)
            start(c, 0, second)
        elif k == 2:
            arrived(c, 0, second)
            for xx in range(NX):
                v = tile_sum(c, 0, xx, y)
                for d in range(2):
                    v = v + buf["rneara"][d, xx].astype(F32) + buf["rmida"][d, xx].astype(F32)
                buf["ua"][xx] = v
            for j in range(3):
                buf["sxa"][j] = buf["ua"][wrap_x(x + j + 1)].astype(BF16)
            start(c, 0, cross)
        else:
            arrived(c, 0, cross)
            v = buf["ua"][x]
            for j in range(3):
                v = v + buf["rxa"][j].astype(F32)
            return v

    def reduce_b(c, k):
        buf = chunks[c]
        if k == 0:
            for j in range(3):
                xx = wrap_x(x + j + 1)
                for yy in range(NY):
                    buf["sxb"][j, yy] = tile_sum(c, 1, xx, yy).astype(BF16)
            start(c, 1, cross)
        elif k == 1:
            arrived(c, 1, cross)
            for yy in range(NY):
                v = tile_sum(c, 1, x, yy)
                for j in range(3):
                    v = v + buf["rxb"][j, yy].astype(F32)
                buf["ub"][yy] = v
            for d in range(2):
                sign = 1 - 2 * d
                buf["sfarb"][d] = buf["ub"][wrap_y(y + 3 * sign)].astype(BF16)
                buf["snearb"][d] = buf["ub"][wrap_y(y + sign)].astype(BF16)
                half = pl.ds(d * half_rows, half_rows)
                buf["shalfb"][d] = buf["ub"][wrap_y(y + 4), half].astype(BF16)
            start(c, 1, first)
        elif k == 2:
            arrived(c, 1, first)
            for d in range(2):
                v = buf["ub"][wrap_y(y + 2 * (1 - 2 * d))] + buf["rfarb"][d].astype(F32)
                parts = [v[:half_rows], v[half_rows:]]
                parts[d] = parts[d] + buf["rhalfb"][d].astype(F32)
                for j in range(2):
                    buf["smidb"][d, j * half_rows : (j + 1) * half_rows] = parts[j].astype(BF16)
            start(c, 1, second)
        else:
            arrived(c, 1, second)
            v = buf["ub"][y]
            for d in range(2):
                v = v + buf["rnearb"][d].astype(F32) + buf["rmidb"][d].astype(F32)
            return v

    gathers = [
        gather_copies(chunks[c]["fa"], chunks[c]["fb"], f_send.at[c], f_recv.at[c])
        for c in range(CHUNKS)
    ]

    def back_copy(c, i):
        peer = lax.rem(me + i, NG)
        return pltpu.make_async_remote_copy(
            src_ref=chunks[c]["picked"].at[peer],
            dst_ref=mg_ref.at[0, me, pl.ds(c * R, R)],
            send_sem=b_send.at[c, i],
            recv_sem=b_recv.at[c, i],
            device_id={"grp": peer},
            device_id_type=MESH,
        )

    def back_own(c):
        return pltpu.make_async_copy(
            chunks[c]["picked"].at[me], mg_ref.at[0, me, pl.ds(c * R, R)], own_sem.at[CHUNKS + c]
        )

    def finish_tile(c):
        buf = chunks[c]
        own_a = reduce_a(c, 3)
        own_b = reduce_b(c, 3)
        rows = pl.ds(c * R, R)
        out_a = (self_term[rows, 0:H] + own_a).astype(BF16)
        out_b = (self_term[rows, H:D] + own_b).astype(BF16)
        gf_ref[rows, 0:H] = out_a
        gf_ref[rows, H:D] = out_b
        buf["fa"][pl.ds(y * NX + x, 1)] = out_a[None]
        buf["fb"][pl.ds(x * NY + y, 1)] = out_b[None]
        gather_stage(gathers[c], 0)

    def send_back(c):
        buf = chunks[c]
        gather_stage(gathers[c], 3)
        for g in range(NG):
            t = tid_ref[g]
            ia = lax.rem(t, NY) * NX + lax.div(t, NY)
            buf["picked"][g, :, 0:H] = buf["fa"][ia]
            buf["picked"][g, :, H:D] = buf["fb"][t]
        back_own(c).start()
        for i in Z_ORDER:
            back_copy(c, i).start()

    stages = []
    for k in range(3):
        def reduce_step(c, k=k):
            if k == 0:
                relay_stage(c)
            reduce_a(c, k)
            reduce_b(c, k)
        stages.append(reduce_step)
    stages.append(finish_tile)
    for k in range(1, 3):
        stages.append(lambda c, k=k: gather_stage(gathers[c], k))
    stages.append(send_back)

    lag = LAG
    for tick in range(len(stages) + lag * (CHUNKS - 1)):
        for c in range(CHUNKS):
            k = tick - lag * c
            if 0 <= k < len(stages):
                stages[k](c)

    for c in range(CHUNKS):
        back_own(c).wait()

        def end(i, carry, c=c):
            z_copy(c, i).wait_send()
            back_copy(c, i).wait()
            return carry

        lax.fori_loop(1, NG, end, 0)
        for color in range(2):
            for n in range(11):
                ring_copy(c, color, n).wait_send()
        gather_finish(gathers[c])


def merge(part, prev, last, tid, grad_out, w_self):
    smem = pl.BlockSpec(memory_space=pltpu.SMEM)
    vmem = pl.BlockSpec(memory_space=pltpu.VMEM)
    hbm = pl.BlockSpec(memory_space=pl.ANY)
    kept = pl.BlockSpec(memory_space=pltpu.HBM)
    half = R // 2
    shapes = dict(
        relay=((NG, 2, R, H), BF16),
        sums=((NG + 1, 2, R, H), F32),
        ua=((NX, R, H), F32),
        ub=((NY, R, H), F32),
        fa=((NE, R, H), BF16),
        fb=((NE, R, H), BF16),
        picked=((NG, R, D), BF16),
    )
    for side in "sr":
        shapes[side + "fara"] = ((2, NX, R, H), BF16)
        shapes[side + "neara"] = ((2, NX, R, H), BF16)
        shapes[side + "halfa"] = ((2, NX // 2, R, H), BF16)
        shapes[side + "mida"] = ((2, NX, R, H), BF16)
        shapes[side + "xa"] = ((3, R, H), BF16)
        shapes[side + "farb"] = ((2, R, H), BF16)
        shapes[side + "nearb"] = ((2, R, H), BF16)
        shapes[side + "halfb"] = ((2, half, H), BF16)
        shapes[side + "midb"] = ((2, R, H), BF16)
        shapes[side + "xb"] = ((3, NY, R, H), BF16)
    per_chunk = [pltpu.VMEM(*shapes[name]) for name in NAMES]
    dma = pltpu.SemaphoreType.DMA
    return pl.pallas_call(
        merge_kernel,
        out_shape=(
            jax.ShapeDtypeStruct((TILE, D), BF16),
            jax.ShapeDtypeStruct((1, NG, TILE, D), BF16),
        ),
        in_specs=[hbm, smem, smem, smem, kept, kept],
        out_specs=(vmem, hbm),
        scratch_shapes=[
            pltpu.VMEM((TILE, D), BF16),
            pltpu.VMEM((D, D), BF16),
            dma((2,)),
            pltpu.VMEM((TILE, D), F32),
            dma((2 * CHUNKS,)),
            dma((CHUNKS, NG)),
            dma((CHUNKS, NG)),
            dma((CHUNKS, 2, 11)),
            dma((CHUNKS, 2, 11)),
            dma((CHUNKS, 2, 11)),
            dma((CHUNKS, 2, 11)),
            dma((CHUNKS, NG)),
            dma((CHUNKS, NG)),
        ]
        + per_chunk * CHUNKS,
        compiler_params=pltpu.CompilerParams(
            collective_id=1, has_side_effects=True, vmem_limit_bytes=VMEM_LIMIT
        ),
        name="merge_mirrors",
    )(part, prev, last, tid, grad_out, w_self)


def per_device(
    grad_out,
    in_degree,
    w_self,
    w_neigh,
    block_dst_tile,
    block_src_group,
    edge_dst,
    edge_src,
    block_count,
    mirror_tiles,
):
    ma, mb, counts, ids, order = gather(
        grad_out,
        in_degree.reshape(1, -1),
        w_neigh,
        edge_src,
        edge_dst,
        mirror_tiles,
        block_src_group.reshape(1, -1),
        block_dst_tile.reshape(1, -1),
        block_count.reshape(1, 1),
    )
    part, prev, last, tid = edge_sums(order, ids, counts, ma, mb)
    return merge(part, prev, last, tid, grad_out, w_self)


def solution(mesh):
    placed = (
        P(("grp", "edge"), None),
        P(("grp", "edge")),
        P(),
        P(),
        P(("grp", "edge")),
        P(("grp", "edge")),
        P(("grp", "edge"), None),
        P(("grp", "edge"), None),
        P(("grp", "edge")),
        P(("grp", "edge"), None),
    )
    return jax.shard_map(
        per_device,
        mesh=mesh,
        in_specs=placed,
        out_specs=(P(("grp", "edge"), None), P(("grp", "edge"), None, None, None)),
        check_vma=False,
    )
```
